32 devices in a mesh: groups: 2 (over x), dp: 4 (over y, core), expert: 4 (over z).
Axes of the slice: x: 2, y: 2, z: 4, core: 2. Of those that a mesh axis runs over, the one named last changes fastest.
Arguments:
- query: bfloat16 [128, 4096], P(('groups', 'dp', 'expert')), parts along dimension 0, may hold values from -27 to 27
- fresh_kv: bfloat16 [128, 512], P(('groups', 'dp', 'expert')), parts along dimension 0, may hold values from -16 to 16
- cache: bfloat16 [128, 512, 512], P(('groups', 'dp', 'expert')), parts along dimension 0, may hold values from -6 to 6
- lengths: int32 [128], P(('groups', 'dp', 'expert')), parts along dimension 0, may hold values from 2 to 512, as said below
- moves: int32 [8, 4], P('groups'), parts along dimension 0, may hold values from 0 to 3, as said below
- residual: bfloat16 [128, 4096], P(('groups', 'dp', 'expert')), parts along dimension 0, may hold values from -4 to 4
- out_weight: bfloat16 [4096, 4096], P('expert'), may hold values from -0.09375 to 0.09375
- norm_gain: float32 [4096], replicated, may hold values from 0.1 to 1.9
- w_gate: bfloat16 [4, 4096, 1536], P('dp', None, 'expert'), may hold values from -0.09375 to 0.09375
- w_up: bfloat16 [4, 4096, 1536], P('dp', None, 'expert'), may hold values from -0.09375 to 0.09375
- w_down: bfloat16 [4, 1536, 4096], P('dp', 'expert'), may hold values from -0.15625 to 0.15625
- routes: int32 [128, 2], P(('groups', 'dp', 'expert')), parts along dimension 0, may hold values from 0 to 3, all different within a row; in each aligned block of 4 rows (0 to 3, 4 to 7, ...) at most 3 rows name the same one
- gates: float32 [128, 2], P(('groups', 'dp', 'expert')), parts along dimension 0, may hold values from 0.05 to 0.5
Outputs:
- layer_out: bfloat16 [128, 4096], P(('groups', 'dp', 'expert')), parts along dimension 0
The draws below stay inside these ranges and needn't reach their ends.
There are 2 independent parts, one for each index of `groups`. The reference program is written for one: setup_inputs(seed, part) draws one part's arguments, and reference() takes and returns one part's arrays. A program takes and returns all parts, laid end to end along the dimension named above; an argument that names none is the same for every part. Nothing has to cross between parts.
Inputs may be any that keep to these rules, and one draw needn't show every extreme that they name: `lengths`: slot 0 of every device (the first of its 4 rows) holds 512 cached positions; other requests 2 to 512. For each expert index e, d -> moves[e, d] is one cycle through all 4 dp indices. `routes`: each row names 2 different experts; in the 4 rows of one device no expert is named by more than 3 rows, and in some device one expert is named by exactly 3.
All inputs are finite; a program needn't handle non-finite values.
Results may differ from the reference program's by a relative error of at most 0.0055.
Values may be sent and summed in bfloat16 or wider, within the bound.
A program may use at most 128 MiB of HBM per device.

```python
import math
import jax
import jax.numpy as jnp
import numpy as np
from jax import lax

D = 4096
HD = 128
QH = 32
KVH = 2
FF = 1536
CTX = 512
REQ_DEV = 4
CAP = 3
EXPERTS = 4
TOP = 2
SLOTS = 64
N_DP = 4
N_EXPERT = 4


def draw_cache(key, part):
    base_draw = jnp.clip(jax.random.normal(jax.random.fold_in(key, 21), (SLOTS, CTX, 2 * KVH * HD), jnp.float32), -6.0, 6.0)
    return base_draw.astype(jnp.bfloat16)


def draw_query(key, part):
    base_draw = jnp.clip(jax.random.normal(jax.random.fold_in(key, 31), (SLOTS, QH * HD), jnp.float32), -6.0, 6.0)
    return base_draw.astype(jnp.bfloat16)


def draw_lengths(key, part):
    drawn = jax.random.randint(jax.random.fold_in(key, 41), (SLOTS,), 2, CTX + 1, jnp.int32)
    return jnp.where(jnp.arange(SLOTS, dtype=jnp.int32) % REQ_DEV == 0, CTX, drawn).astype(jnp.int32)


def draw_moves(key, part):
    key_list = jax.random.split(jax.random.fold_in(key, 51), N_EXPERT)
    orders = jax.vmap(lambda single: jax.random.permutation(single, N_DP))(key_list).astype(jnp.int32)
    shifted = jnp.roll(orders, -1, axis=1)
    row_ids = jnp.arange(N_EXPERT, dtype=jnp.int32)[:, None]
    return jnp.zeros((N_EXPERT, N_DP), jnp.int32).at[row_ids, orders].set(shifted)


def level_of(rng, dims, shards, least, top_value):
    def one(position, parts):
        heights = jax.random.uniform(jax.random.fold_in(jax.random.fold_in(rng, 6), position), (parts,), jnp.float32, least / len(shards), top_value / len(shards))
        return jnp.repeat(jnp.exp(heights), dims[position] // parts).reshape((-1,) + (1,) * (len(dims) - position - 1))

    level = one(*shards[0])
    for cut in shards[1:]:
        level = level * one(*cut)
    return level


def deal_out(own_key, own, number, rows, count, top, reach, lean):
    order = jax.random.permutation(own_key, count)
    crowded, common = shares(count, rows * top, reach, lean, True), shares(count, rows * top, reach, lean, False)
    places = jnp.arange(count)

    def named(tallies, rotation):
        used = int((tallies > 0).sum())
        fixed = max(1, used // 4)
        moved = fixed + (places - fixed + rotation * (used - fixed)) % max(1, count - fixed)
        return jnp.zeros((count,), jnp.int32).at[order[jnp.where(places < fixed, places, moved)]].set(jnp.asarray(tallies, jnp.int32))

    tallies = jnp.where(number % 4 == 0, named(crowded, number // 4), named(common, number - number // 4 - 1))
    mixed = jax.random.permutation(jax.random.fold_in(own, 3), count)
    giver, receiver = mixed[0:count // 2 * 2:2], mixed[1:count // 2 * 2:2]
    margin = jnp.minimum(tallies[giver] - 1, reach - tallies[receiver]) // 2
    margin = jnp.where((giver == order[0]) | (receiver == order[0]) | (tallies[receiver] == 0), 0, jnp.maximum(margin, 0))
    moved = jax.random.randint(jax.random.fold_in(own, 4), (count // 2,), 0, 1 << 20) % (margin + 1)
    tallies = tallies.at[giver].add(-moved).at[receiver].add(moved)
    items = jnp.searchsorted(jnp.cumsum(tallies), jnp.arange(rows * top), side="right").astype(jnp.int32)
    listing = items.reshape(top, rows).T
    listing = listing[jax.random.permutation(jax.random.fold_in(own, 1), rows)]
    rotation = jax.random.randint(jax.random.fold_in(own, 2), (rows, 1), 0, top)
    return jnp.take_along_axis(listing, (jnp.arange(top)[None, :] + rotation) % top, axis=1)


def shares(amount, total, most, lean, full):
    loads = [(1 << 20) // math.isqrt(grade ** lean) + 1 for grade in range(1, amount + 1)]
    largest = most if full else min(most, max(-(-total // amount), total * loads[0] // sum(loads)))
    least = 1 if total - largest >= amount - 1 else 0
    holding, surplus = [largest] + [least] * (amount - 1), total - largest - least * (amount - 1)
    while surplus > 0:
        movable = [i for i in range(1, amount) if holding[i] < largest] or [i for i in range(1, amount) if holding[i] < most]
        pool, left = sum([loads[i] for i in movable]), surplus
        for i in movable:
            extra = min(most - holding[i], max(1, left * loads[i] // pool), surplus)
            holding[i] = holding[i] + extra
            surplus = surplus - extra
    return np.array(holding)


def gaussian(key, extent, deviation, most, cuts=(), kind=jnp.bfloat16):
    result = jax.random.normal(key, extent, jnp.float32) * deviation
    if len(cuts) > 0:
        result = level_of(key, extent, cuts, -0.22, 0.18) * result
    return jnp.clip(result, min=-most, max=most).astype(kind)


def setup_inputs(seed: int = 0, part: int = 0) -> dict:
    streams_of = jax.random.split(jax.random.key(seed), 14)
    part_splits = jax.random.split(jax.random.fold_in(streams_of[13], part), 14)
    query = draw_query(jax.random.fold_in(jax.random.fold_in(streams_of[13], part), 71), part)
    fresh_kv = gaussian(part_splits[1], (SLOTS, 2 * KVH * HD), 3.0, 16.0, ((0, 16),))
    cache = draw_cache(jax.random.fold_in(jax.random.fold_in(streams_of[13], part), 71), part)
    lengths = draw_lengths(jax.random.fold_in(jax.random.fold_in(streams_of[13], part), 71), part)
    moves = draw_moves(jax.random.fold_in(jax.random.fold_in(streams_of[13], part), 71), part)
    residual = gaussian(part_splits[5], (SLOTS, D), 0.5, 4.0, ((0, 16),))
    out_weight = gaussian(streams_of[6], (QH * HD, D), (QH * HD) ** -0.5, 0.09375, ((0, 4),))
    norm_gain = jnp.clip(1.0 + 0.18 * jax.random.normal(streams_of[7], (D,), jnp.float32), 0.1, 1.9)
    w_gate = gaussian(streams_of[8], (EXPERTS, D, FF), D ** -0.5, 0.09375, ((0, 4), (2, 4)))
    w_up = gaussian(streams_of[9], (EXPERTS, D, FF), D ** -0.5, 0.09375, ((0, 4), (2, 4)))
    w_down = gaussian(streams_of[10], (EXPERTS, FF, D), FF ** -0.5, 0.15625, ((0, 4), (1, 4)))
    routes_keys = jax.random.split(jax.random.fold_in(part_splits[11], 1), SLOTS // REQ_DEV)
    routes_turns = jax.random.permutation(jax.random.fold_in(part_splits[11], 3), SLOTS // REQ_DEV)
    routes = jax.vmap(lambda own, number: deal_out(jax.random.fold_in(part_splits[11], 2), own, number, REQ_DEV, EXPERTS, TOP, CAP, 2))(routes_keys, routes_turns).reshape((SLOTS, TOP))
    gates = jnp.clip(jnp.exp(math.log(0.5) - 2.3025851 * jax.random.uniform(part_splits[12], (SLOTS, TOP), jnp.float32) ** level_of(part_splits[12], (SLOTS, TOP), ((0, 16),), -0.2, 0.2)), 0.05, 0.5)
    return dict(query=query, fresh_kv=fresh_kv, cache=cache, lengths=lengths, moves=moves, residual=residual, out_weight=out_weight, norm_gain=norm_gain, w_gate=w_gate, w_up=w_up, w_down=w_down, routes=routes, gates=gates)


norm_eps = 1e-06

def cache_part(queries, entries, lengths_used):
    count_rows = queries.shape[0]
    group_size = QH // KVH
    query_heads = queries.astype(jnp.float32).reshape(count_rows, KVH, group_size, HD)
    keys_all = entries[:, :, :KVH * HD].astype(jnp.float32).reshape(count_rows, CTX, KVH, HD)
    values_all = entries[:, :, KVH * HD:].astype(jnp.float32).reshape(count_rows, CTX, KVH, HD)
    scores = jnp.einsum('nhgd,nchd->nhgc', query_heads, keys_all) * HD ** (-0.5)
    valid_mask = (jnp.arange(CTX, dtype=jnp.int32)[None, :] < lengths_used[:, None])[:, None, None, :]
    scores = jnp.where(valid_mask, scores, -1e+30)
    row_max = lax.optimization_barrier(jnp.max(scores, axis=-1))
    weights_raw = jnp.where(valid_mask, jnp.exp(scores - row_max[..., None]), 0.0)
    row_sum = lax.optimization_barrier(jnp.sum(weights_raw, axis=-1))
    rounded = lax.optimization_barrier(weights_raw.astype(jnp.bfloat16)).astype(jnp.float32)
    out_cache = jnp.einsum('nhgc,nchd->nhgd', rounded, values_all)
    return (out_cache.reshape(count_rows, QH * HD), row_max.reshape(count_rows, QH), row_sum.reshape(count_rows, QH))

def combine_own(out_cache, row_max, row_sum, queries, fresh):
    count_rows = queries.shape[0]
    group_size = QH // KVH
    query_heads = queries.astype(jnp.float32).reshape(count_rows, KVH, group_size, HD)
    own_keys = fresh[:, :KVH * HD].astype(jnp.float32).reshape(count_rows, KVH, 1, HD)
    own_values = fresh[:, KVH * HD:].astype(jnp.float32).reshape(count_rows, KVH, 1, HD)
    own_score = lax.optimization_barrier(jnp.sum(query_heads * own_keys, axis=-1)) * HD ** (-0.5)
    max_heads = row_max.reshape(count_rows, KVH, group_size)
    sum_heads = row_sum.reshape(count_rows, KVH, group_size)
    top_score = jnp.maximum(max_heads, own_score)
    cache_factor = jnp.exp(max_heads - top_score)
    own_factor = jnp.exp(own_score - top_score)
    numer = cache_factor[..., None] * out_cache.reshape(count_rows, KVH, group_size, HD) + own_factor[..., None] * own_values
    denom = cache_factor * sum_heads + own_factor
    return (numer / denom[..., None]).reshape(count_rows, QH * HD).astype(jnp.bfloat16)

def reference(query, fresh_kv, cache, lengths, moves, residual, out_weight, norm_gain, w_gate, w_up, w_down, routes, gates):
    slot_ids = jnp.arange(SLOTS, dtype=jnp.int32)
    local_ids = slot_ids % REQ_DEV
    device_ids = slot_ids // REQ_DEV
    dp_ids = device_ids // N_EXPERT
    ex_ids = device_ids % N_EXPERT
    target = moves[ex_ids, dp_ids].astype(jnp.int32)
    new_of_old = jnp.where(local_ids == 0, (target * N_EXPERT + ex_ids) * REQ_DEV, slot_ids).astype(jnp.int32)
    old_of_new = jnp.zeros((SLOTS,), jnp.int32).at[new_of_old].set(slot_ids)
    query_old = query[new_of_old]
    block_count = SLOTS // REQ_DEV

    def one_block(items):
        return cache_part(items[0], items[1], items[2])
    out_all, max_all, sum_all = lax.map(one_block, (query_old.reshape(block_count, REQ_DEV, QH * HD), cache.reshape(block_count, REQ_DEV, CTX, 2 * KVH * HD), lengths.reshape(block_count, REQ_DEV)))
    out_new = out_all.reshape(SLOTS, QH * HD)[old_of_new]
    max_new = max_all.reshape(SLOTS, QH)[old_of_new]
    sum_new = sum_all.reshape(SLOTS, QH)[old_of_new]
    attended = combine_own(out_new, max_new, sum_new, query, fresh_kv)
    projected = jnp.dot(attended, out_weight, preferred_element_type=jnp.float32)
    hidden = residual.astype(jnp.float32) + projected
    normed = (hidden * lax.rsqrt(lax.optimization_barrier(jnp.mean(hidden * hidden, axis=-1, keepdims=True)) + norm_eps) * norm_gain.astype(jnp.float32)).astype(jnp.bfloat16)

    def expert_step(total, items):
        gate_w, up_w, down_w, expert_id = items
        gate_val = jnp.dot(normed, gate_w, preferred_element_type=jnp.float32)
        up_val = jnp.dot(normed, up_w, preferred_element_type=jnp.float32)
        activation = (jax.nn.silu(gate_val) * up_val).astype(jnp.bfloat16)
        expert_out = jnp.dot(activation, down_w, preferred_element_type=jnp.float32)
        weight_sel = lax.optimization_barrier(jnp.sum(jnp.where(routes == expert_id, gates.astype(jnp.float32), 0.0), axis=-1))
        return (total + weight_sel[:, None] * expert_out, None)
    mixture, _ = lax.scan(expert_step, jnp.zeros((SLOTS, D), jnp.float32), (w_gate, w_up, w_down, jnp.arange(EXPERTS, dtype=jnp.int32)))
    return (hidden + mixture).astype(jnp.bfloat16)
```

```python
import functools

import jax
import jax.numpy as jnp
from jax import lax
from jax.experimental import pallas as pl
from jax.experimental.pallas import tpu as pltpu
from jax.sharding import PartitionSpec as P

HD = 128
KVH = 2
NORM_EPS = 1e-06
F32 = jnp.float32
BF16 = jnp.bfloat16


def layer_kernel(
    dp,
    ex,
    lengths,
    moves,
    query,
    fresh,
    residual,
    routes,
    gates,
    gain,
    cache_hbm,
    wo_hbm,
    wg_hbm,
    wu_hbm,
    wd_hbm,
    out,
    cache,
    wo,
    wg,
    wu,
    wd,
    qf,
    q_send,
    q_recv,
    r_send,
    r_recv,
    a_send,
    a0_send,
    a0_recv,
    a_recv,
    a_all,
    p_send,
    p_recv,
    hid,
    x_send,
    s_send,
    x_all,
    s_all,
    y_send,
    y_recv,
    total,
    fold,
    z_send,
    z_recv,
    local_sem,
    q_s,
    q_r,
    r_s,
    r_r,
    a_s,
    a_r,
    a0_s,
    a0_r,
    p_s,
    p_r,
    x_s,
    x_r,
    s_s,
    s_r,
    x2_s,
    x2_r,
    s2_s,
    s2_r,
    y_s,
    y_r,
    z_s,
    z_r,
):
    d = lax.axis_index("dp")
    e = lax.axis_index("expert")
    n = dp * ex
    me = d * ex + e
    rows = query.shape[0]
    width = query.shape[1]
    heads = width // HD
    group = heads // KVH
    hk = heads // ex
    ctx = cache.shape[1]
    part = width // ex
    tiles = part // HD
    tokens = rows * ex
    top = routes.shape[1]
    pieces = 16 // rows
    piece = width // pieces

    def copy(src, dst, ss, rs, dd, ee):
        return pltpu.make_async_remote_copy(
            src_ref=src,
            dst_ref=dst,
            send_sem=ss,
            recv_sem=rs,
            device_id={"dp": dd, "expert": ee},
            device_id_type=pl.DeviceIdType.MESH,
        )

    barrier = pltpu.get_barrier_semaphore()

    def greet(o, c):
        p = lax.rem(me + o, n)
        pl.semaphore_signal(
            barrier,
            inc=1,
            device_id={"dp": p // ex, "expert": lax.rem(p, ex)},
            device_id_type=pl.DeviceIdType.MESH,
        )
        return c

    lax.fori_loop(1, n, greet, 0)

    local = [
        pltpu.make_async_copy(cache_hbm, cache, local_sem.at[0]),
        pltpu.make_async_copy(wo_hbm, wo, local_sem.at[1]),
        pltpu.make_async_copy(wg_hbm.at[0], wg, local_sem.at[2]),
        pltpu.make_async_copy(wu_hbm.at[0], wu, local_sem.at[3]),
        pltpu.make_async_copy(wd_hbm.at[0], wd, local_sem.at[4]),
    ]
    for c in local:
        c.start()

    for h in range(heads):
        qf[:, h, :] = query[:, h * HD : (h + 1) * HD].astype(F32)
    for i in range(2 * KVH):
        qf[:, heads + i, :] = fresh[:, i * HD : (i + 1) * HD].astype(F32)
    pad = qf.shape[1] - heads - 2 * KVH
    qf[:, heads + 2 * KVH :, :] = jnp.zeros((rows, pad, HD), F32)
    q_send[...] = qf[0].astype(BF16)

    lane = lax.broadcasted_iota(jnp.int32, (rows, HD), 1)
    table = jnp.zeros((rows, HD), F32)
    for k in range(top):
        table += jnp.where(lane == routes[:, k : k + 1], gates[:, k : k + 1], 0.0)
    for k in range(ex):
        for j in range(tiles):
            r_send[k, :, j, :] = residual[
                :, k * part + j * HD : k * part + (j + 1) * HD
            ].astype(F32)
        r_send[k, :, tiles, :] = table

    pl.semaphore_wait(barrier, n - 1)

    sends = []

    def exchange(count, me_, make):
        made = [make(lax.rem(me_ + o, count)) for o in range(1, count)]
        for c in made:
            c.start()
        sends.extend(made)

    exchange(dp, d, lambda p: copy(q_send, q_recv.at[d], q_s.at[p], q_r.at[d], p, e))
    exchange(
        ex,
        e,
        lambda p: copy(
            r_send.at[p], r_recv.at[pl.ds(e * rows, rows)], r_s.at[p], r_r.at[e], d, p
        ),
    )
    q_recv[d] = q_send[...]
    r_recv[pl.ds(e * rows, rows)] = r_send[e]

    head = lax.broadcasted_iota(jnp.int32, (heads, 1), 0)
    first = head < group

    def attend(r, q_all):
        q = q_all[:heads]
        own_key = jnp.where(first, q_all[heads : heads + 1], q_all[heads + 1 : heads + 2])
        own_value = jnp.where(
            first, q_all[heads + 2 : heads + 3], q_all[heads + 3 : heads + 4]
        )
        wide = jnp.concatenate(
            [jnp.where(first, q, 0.0), jnp.where(first, 0.0, q)], axis=1
        ).astype(BF16)
        scores = lax.dot_general(
            wide,
            cache[r, :, : KVH * HD],
            (((1,), (1,)), ((), ())),
            preferred_element_type=F32,
        ) * HD ** (-0.5)
        position = lax.broadcasted_iota(jnp.int32, (heads, ctx), 1)
        valid = position < lengths[r]
        scores = jnp.where(valid, scores, -1e30)
        cache_max = jnp.max(scores, axis=-1, keepdims=True)
        weights = jnp.where(valid, jnp.exp(scores - cache_max), 0.0)
        cache_sum = jnp.sum(weights, axis=-1, keepdims=True)
        both = jnp.dot(
            weights.astype(BF16), cache[r, :, KVH * HD :], preferred_element_type=F32
        )
        cache_out = jnp.where(first, both[:, :HD], both[:, HD:])
        own_score = jnp.sum(q * own_key, axis=-1, keepdims=True) * HD ** (-0.5)
        top_score = jnp.maximum(cache_max, own_score)
        f_cache = jnp.exp(cache_max - top_score)
        f_own = jnp.exp(own_score - top_score)
        return (f_cache * cache_out + f_own * own_value) / (f_cache * cache_sum + f_own)

    local[0].wait()

    def stay(r, c):
        att = attend(r, qf[r])
        for k in range(ex):
            a_send[k, r - 1] = att[k * hk : (k + 1) * hk]
        return c

    lax.fori_loop(1, rows, stay, 0)
    exchange(
        ex,
        e,
        lambda p: copy(
            a_send.at[p],
            a_recv.at[pl.ds(e * rows + 1, rows - 1)],
            a_s.at[p],
            a_r.at[e],
            d,
            p,
        ),
    )
    a_recv[pl.ds(e * rows + 1, rows - 1)] = a_send[e]

    for o in range(1, dp):
        p = lax.rem(d + o, dp)
        copy(q_send, q_recv.at[p], q_s.at[p], q_r.at[p], p, e).wait_recv()
    target = moves[e, d]
    q0 = jnp.zeros(q_send.shape, F32)
    for j in range(dp):
        q0 += jnp.where(target == j, q_recv[j].astype(F32), 0.0)
    att = attend(0, q0)
    for k in range(ex):
        a0_send[k] = att[k * hk : (k + 1) * hk]

    def a0_copy(o, source):
        p = lax.rem(me + o, n)
        pd, pk = p // ex, lax.rem(p, ex)
        sd, sk = (d, e) if not source else (pd, pk)
        slot = me if not source else p
        return copy(
            a0_send.at[pk], a0_recv.at[sd, sk], a0_s.at[p], a0_r.at[slot], pd, pk
        )

    def a0_start(o, c):
        a0_copy(o, False).start()
        return c

    lax.fori_loop(1, n, a0_start, 0)
    a0_recv[d, e] = a0_send[e]

    for o in range(1, ex):
        p = lax.rem(e + o, ex)
        copy(
            r_send.at[p], r_recv.at[pl.ds(p * rows, rows)], r_s.at[p], r_r.at[p], d, p
        ).wait_recv()
        copy(
            a_send.at[p],
            a_recv.at[pl.ds(p * rows + 1, rows - 1)],
            a_s.at[p],
            a_r.at[p],
            d,
            p,
        ).wait_recv()

    def a0_wait(o, c):
        a0_copy(o, True).wait_recv()
        return c

    local[1].wait()
    lax.fori_loop(1, n, a0_wait, 0)
    for k in range(ex):
        chosen = jnp.zeros((hk, HD), F32)
        for j in range(dp):
            chosen += jnp.where(moves[k, j] == d, a0_recv[j, k], 0.0)
        a_recv[k * rows] = chosen
    for h in range(hk):
        a_all[:, h * HD : (h + 1) * HD] = a_recv[:, h, :].astype(BF16)

    def project(k):
        return jnp.dot(
            a_all[...],
            wo[:, pl.ds(pl.multiple_of(k * part, HD), part)],
            preferred_element_type=F32,
        )

    for o in range(1, ex):
        p = lax.rem(e + o, ex)
        p_send[p] = project(p).astype(BF16)
        c = copy(p_send.at[p], p_recv.at[e], p_s.at[p], p_r.at[e], d, p)
        c.start()
        sends.append(c)
    hid[...] = project(e)
    for j in range(tiles):
        hid[:, j * HD : (j + 1) * HD] += r_recv[:, j, :]
    for o in range(1, ex):
        p = lax.rem(e + o, ex)
        copy(p_send.at[p], p_recv.at[p], p_s.at[p], p_r.at[p], d, p).wait_recv()
        hid[...] += p_recv[p].astype(F32)

    hidden = hid[...]
    squares = jnp.sum(hidden * hidden, axis=-1, keepdims=True)
    last = lax.broadcasted_iota(jnp.int32, (tokens, HD), 1) == HD - 1
    s_send[...] = jnp.where(last, squares, r_recv[:, tiles, :])
    x_send[...] = (
        hidden * gain[:, pl.ds(pl.multiple_of(e * part, HD), part)]
    ).astype(BF16)

    def x_at(dd, ee):
        return x_all.at[
            pl.ds(pl.multiple_of(dd * tokens, 16), tokens),
            pl.ds(pl.multiple_of(ee * part, HD), part),
        ]

    exchange(ex, e, lambda p: copy(x_send, x_at(d, e), x_s.at[p], x_r.at[e], d, p))
    exchange(
        ex, e, lambda p: copy(s_send, s_all.at[d, e], s_s.at[p], s_r.at[e], d, p)
    )
    x_at(d, e)[...] = x_send[...]
    s_all[d, e] = s_send[...]
    for o in range(1, ex):
        p = lax.rem(e + o, ex)
        copy(x_send, x_at(d, p), x_s.at[p], x_r.at[p], d, p).wait_recv()
        copy(s_send, s_all.at[d, p], s_s.at[p], s_r.at[p], d, p).wait_recv()

    def x_rows(dd):
        return x_all.at[pl.ds(pl.multiple_of(dd * tokens, 16), tokens)]

    exchange(dp, d, lambda p: copy(x_rows(d), x_rows(d), x2_s.at[p], x2_r.at[d], p, e))
    exchange(
        dp, d, lambda p: copy(s_all.at[d], s_all.at[d], s2_s.at[p], s2_r.at[d], p, e)
    )
    local[2].wait()
    local[3].wait()
    for o in range(1, dp):
        p = lax.rem(d + o, dp)
        copy(x_rows(p), x_rows(p), x2_s.at[p], x2_r.at[p], p, e).wait_recv()
        copy(s_all.at[p], s_all.at[p], s2_s.at[p], s2_r.at[p], p, e).wait_recv()

    every = dp * tokens
    wide_lane = lax.broadcasted_iota(jnp.int32, (every, HD), 1)
    stats = s_all[:, 0].reshape(every, HD)
    weight = jnp.sum(jnp.where(wide_lane == d, stats, 0.0), axis=-1, keepdims=True)
    for k in range(1, ex):
        stats += s_all[:, k].reshape(every, HD)
    mean = (
        jnp.sum(jnp.where(wide_lane == HD - 1, stats, 0.0), axis=-1, keepdims=True)
        / width
    )
    scale = lax.rsqrt(mean + NORM_EPS)
    gate_val = jnp.dot(x_all[...], wg[...], preferred_element_type=F32) * scale
    up_val = jnp.dot(x_all[...], wu[...], preferred_element_type=F32) * scale
    act = (gate_val / (1.0 + jnp.exp(-gate_val)) * up_val).astype(BF16)

    local[4].wait()

    def y_copy(p, src, c):
        cols = pl.ds(c * part, part)
        return copy(
            y_send.at[p, :, cols],
            y_recv.at[src, :, cols],
            y_s.at[c, p],
            y_r.at[c, src],
            p,
            e,
        )

    for c in range(ex):
        y = jnp.dot(
            act, wd[:, c * part : (c + 1) * part], preferred_element_type=F32
        )
        y_send[:, :, c * part : (c + 1) * part] = (
            (y * weight).astype(BF16).reshape(dp, tokens, part)
        )
        exchange(dp, d, lambda p, c=c: y_copy(p, d, c))
    for c in range(ex):
        cols = slice(c * part, (c + 1) * part)
        got = y_send[d, :, cols].astype(F32)
        for o in range(1, dp):
            p = lax.rem(d + o, dp)
            y_copy(p, p, c).wait_recv()
            got += y_recv[p, :, cols].astype(F32)
        total[:, cols] = got
    total[:, pl.ds(pl.multiple_of(e * part, HD), part)] += hid[...]

    for k in range(ex):
        for c in range(pieces):
            fold[k, c * rows : (c + 1) * rows, :] = total[
                k * rows : (k + 1) * rows, c * piece : (c + 1) * piece
            ]
        z_send[k] = fold[k].astype(BF16)
    exchange(
        ex, e, lambda p: copy(z_send.at[p], z_recv.at[e], z_s.at[p], z_r.at[e], d, p)
    )
    result = fold[e]
    for o in range(1, ex):
        p = lax.rem(e + o, ex)
        copy(z_send.at[p], z_recv.at[p], z_s.at[p], z_r.at[p], d, p).wait_recv()
        result += z_recv[p].astype(F32)
    for c in range(pieces):
        out[:, c * piece : (c + 1) * piece] = result[c * rows : (c + 1) * rows].astype(
            out.dtype
        )

    for c in sends:
        c.wait_send()

    def a0_sent(o, c):
        a0_copy(o, False).wait_send()
        return c

    lax.fori_loop(1, n, a0_sent, 0)


def per_device(
    query,
    fresh_kv,
    cache,
    lengths,
    moves,
    residual,
    out_weight,
    norm_gain,
    w_gate,
    w_up,
    w_down,
    routes,
    gates,
):
    dp = lax.axis_size("dp")
    ex = lax.axis_size("expert")
    n = dp * ex
    rows, width = query.shape
    heads = width // HD
    hk = heads // ex
    part = width // ex
    tiles = part // HD
    tokens = rows * ex
    ff = w_gate.shape[-1]
    pieces = 16 // rows
    qrows = -(-(heads + 2 * KVH) // 16) * 16
    dma = pltpu.SemaphoreType.DMA
    vmem = pltpu.VMEM
    scratch = [
        vmem(cache.shape, BF16),
        vmem(out_weight.shape, BF16),
        vmem((width, ff), BF16),
        vmem((width, ff), BF16),
        vmem((ff, width), BF16),
        vmem((rows, qrows, HD), F32),
        vmem((qrows, HD), BF16),
        vmem((dp, qrows, HD), BF16),
        vmem((ex, rows, tiles + 1, HD), F32),
        vmem((tokens, tiles + 1, HD), F32),
        vmem((ex, rows - 1, hk, HD), F32),
        vmem((ex, hk, HD), F32),
        vmem((dp, ex, hk, HD), F32),
        vmem((tokens, hk, HD), F32),
        vmem((tokens, part), BF16),
        vmem((ex, tokens, part), BF16),
        vmem((ex, tokens, part), BF16),
        vmem((tokens, part), F32),
        vmem((tokens, part), BF16),
        vmem((tokens, HD), F32),
        vmem((dp * tokens, width), BF16),
        vmem((dp, ex, tokens, HD), F32),
        vmem((dp, tokens, width), BF16),
        vmem((dp, tokens, width), BF16),
        vmem((tokens, width), F32),
        vmem((ex, 16, width // pieces), F32),
        vmem((ex, 16, width // pieces), BF16),
        vmem((ex, 16, width // pieces), BF16),
        dma((5,)),
    ]
    for shape in (
        (dp,),
        (ex,),
        (ex,),
        (n,),
        (ex,),
        (ex,),
        (ex,),
        (dp,),
        (dp,),
        (ex, dp),
        (ex,),
    ):
        scratch += [dma(shape), dma(shape)]
    smem = pl.BlockSpec(memory_space=pltpu.SMEM)
    inside = pl.BlockSpec(memory_space=pltpu.VMEM)
    outside = pl.BlockSpec(memory_space=pl.ANY)
    return pl.pallas_call(
        functools.partial(layer_kernel, dp, ex),
        out_shape=jax.ShapeDtypeStruct(query.shape, BF16),
        in_specs=[smem] * 2 + [inside] * 6 + [outside] * 5,
        out_specs=inside,
        scratch_shapes=scratch,
        compiler_params=pltpu.CompilerParams(
            collective_id=0,
            has_side_effects=True,
            vmem_limit_bytes=56 * 1024 * 1024,
        ),
    )(
        lengths,
        moves,
        query,
        fresh_kv,
        residual,
        routes,
        gates,
        norm_gain.reshape(1, width),
        cache,
        out_weight,
        w_gate,
        w_up,
        w_down,
    )


def solution(mesh):
    placed = (
        P(("groups", "dp", "expert"), None),
        P(("groups", "dp", "expert"), None),
        P(("groups", "dp", "expert"), None, None),
        P(("groups", "dp", "expert")),
        P("groups", None),
        P(("groups", "dp", "expert"), None),
        P("expert", None),
        P(),
        P("dp", None, "expert"),
        P("dp", None, "expert"),
        P("dp", "expert", None),
        P(("groups", "dp", "expert"), None),
        P(("groups", "dp", "expert"), None),
    )
    return jax.shard_map(
        per_device,
        mesh=mesh,
        in_specs=placed,
        out_specs=P(("groups", "dp", "expert"), None),
        check_vma=False,
    )
```

```python
import functools

import jax
import jax.numpy as jnp
from jax import lax
from jax.experimental import pallas as pl
from jax.experimental.pallas import tpu as pltpu
from jax.sharding import PartitionSpec as P

HD = 128
KVH = 2
NORM_EPS = 1e-06
F32 = jnp.float32
BF16 = jnp.bfloat16


def layer_kernel(
    dp,
    ex,
    lengths,
    moves,
    routes,
    gates,
    query,
    fresh,
    residual,
    gain,
    cache_hbm,
    wo_hbm,
    wg_hbm,
    wu_hbm,
    wd_hbm,
    out,
    cache,
    wo,
    wg,
    wu,
    wd,
    qf,
    q_send,
    q_recv,
    r_send,
    r_recv,
    a_send,
    a0_send,
    a0_recv,
    a_recv,
    a_all,
    p_send,
    p_recv,
    hid,
    x_send,
    s_send,
    s_part,
    x_all,
    s_all,
    gate_sum,
    up_sum,
    y_send,
    y_recv,
    v_send,
    v_recv,
    total,
    fold,
    z_send,
    z_recv,
    local_sem,
    q_s,
    q_r,
    r_s,
    r_r,
    a_s,
    a_r,
    a0_s,
    a0_r,
    p_s,
    p_r,
    x_s,
    x_r,
    s_s,
    s_r,
    x2_s,
    x2_r,
    x3_s,
    s2_s,
    s2_r,
    y_s,
    y_r,
    v_s,
    v_r,
    z_s,
    z_r,
):
    d = lax.axis_index("dp")
    e = lax.axis_index("expert")
    n = dp * ex
    me = d * ex + e
    rows = query.shape[0]
    width = query.shape[1]
    heads = width // HD
    group = heads // KVH
    hk = heads // ex
    ctx = cache.shape[1]
    part = width // ex
    tiles = part // HD
    tokens = rows * ex
    top = routes.shape[0]
    pieces = 16 // rows
    piece = part // pieces

    def copy(src, dst, ss, rs, dd, ee):
        return pltpu.make_async_remote_copy(
            src_ref=src,
            dst_ref=dst,
            send_sem=ss,
            recv_sem=rs,
            device_id={"dp": dd, "expert": ee},
            device_id_type=pl.DeviceIdType.MESH,
        )

    barrier = pltpu.get_barrier_semaphore()

    def greet(o, c):
        p = lax.rem(me + o, n)
        pl.semaphore_signal(
            barrier,
            inc=1,
            device_id={"dp": p // ex, "expert": lax.rem(p, ex)},
            device_id_type=pl.DeviceIdType.MESH,
        )
        return c

    lax.fori_loop(1, n, greet, 0)

    local = [
        pltpu.make_async_copy(cache_hbm, cache, local_sem.at[0]),
        pltpu.make_async_copy(wo_hbm, wo, local_sem.at[1]),
        pltpu.make_async_copy(wg_hbm.at[0], wg, local_sem.at[2]),
        pltpu.make_async_copy(wu_hbm.at[0], wu, local_sem.at[3]),
        pltpu.make_async_copy(wd_hbm.at[0], wd, local_sem.at[4]),
    ]
    for c in local:
        c.start()

    for h in range(heads):
        qf[:, h, :] = query[:, h * HD : (h + 1) * HD].astype(F32)
    for i in range(2 * KVH):
        qf[:, heads + i, :] = fresh[:, i * HD : (i + 1) * HD].astype(F32)
    pad = qf.shape[1] - heads - 2 * KVH
    qf[:, heads + 2 * KVH :, :] = jnp.zeros((rows, pad, HD), F32)
    q_send[...] = qf[0].astype(BF16)

    lane = lax.broadcasted_iota(jnp.int32, (rows, HD), 1)
    line = lax.broadcasted_iota(jnp.int32, (rows, HD), 0)
    table = jnp.zeros((rows, HD), F32)
    for r in range(rows):
        for k in range(top):
            named = (line == r) & (lane == routes[k, r])
            table += jnp.where(named, gates[k, r], 0.0)
    for k in range(ex):
        for j in range(tiles):
            r_send[k, :, j, :] = residual[
                :, k * part + j * HD : k * part + (j + 1) * HD
            ].astype(F32)
        r_send[k, :, tiles, :] = table

    pl.semaphore_wait(barrier, n - 1)

    sends = []

    def exchange(count, me_, make):
        made = [make(lax.rem(me_ + o, count)) for o in range(1, count)]
        for c in made:
            c.start()
        sends.extend(made)

    exchange(dp, d, lambda p: copy(q_send, q_recv.at[d], q_s.at[p], q_r.at[d], p, e))
    exchange(
        ex,
        e,
        lambda p: copy(
            r_send.at[p], r_recv.at[pl.ds(e * rows, rows)], r_s.at[p], r_r.at[e], d, p
        ),
    )
    q_recv[d] = q_send[...]
    r_recv[pl.ds(e * rows, rows)] = r_send[e]

    head = lax.broadcasted_iota(jnp.int32, (heads, 1), 0)
    first = head < group

    def attend(r, q_all):
        q = q_all[:heads]
        own_key = jnp.where(first, q_all[heads : heads + 1], q_all[heads + 1 : heads + 2])
        own_value = jnp.where(
            first, q_all[heads + 2 : heads + 3], q_all[heads + 3 : heads + 4]
        )
        wide = jnp.concatenate(
            [jnp.where(first, q, 0.0), jnp.where(first, 0.0, q)], axis=1
        ).astype(BF16)
        scores = lax.dot_general(
            wide,
            cache[r, :, : KVH * HD],
            (((1,), (1,)), ((), ())),
            preferred_element_type=F32,
        ) * HD ** (-0.5)
        position = lax.broadcasted_iota(jnp.int32, (heads, ctx), 1)
        valid = position < lengths[r]
        scores = jnp.where(valid, scores, -1e30)
        cache_max = jnp.max(scores, axis=-1, keepdims=True)
        weights = jnp.where(valid, jnp.exp(scores - cache_max), 0.0)
        cache_sum = jnp.sum(weights, axis=-1, keepdims=True)
        both = jnp.dot(
            weights.astype(BF16), cache[r, :, KVH * HD :], preferred_element_type=F32
        )
        cache_out = jnp.where(first, both[:, :HD], both[:, HD:])
        own_score = jnp.sum(q * own_key, axis=-1, keepdims=True) * HD ** (-0.5)
        top_score = jnp.maximum(cache_max, own_score)
        f_cache = jnp.exp(cache_max - top_score)
        f_own = jnp.exp(own_score - top_score)
        return (f_cache * cache_out + f_own * own_value) / (f_cache * cache_sum + f_own)

    local[0].wait()

    for r in range(1, rows):
        att = attend(r, qf[r])
        for k in range(ex):
            a_send[k, r - 1] = att[k * hk : (k + 1) * hk]
    exchange(
        ex,
        e,
        lambda p: copy(
            a_send.at[p],
            a_recv.at[pl.ds(e * rows + 1, rows - 1)],
            a_s.at[p],
            a_r.at[e],
            d,
            p,
        ),
    )
    a_recv[pl.ds(e * rows + 1, rows - 1)] = a_send[e]

    for o in range(1, dp):
        p = lax.rem(d + o, dp)
        copy(q_send, q_recv.at[p], q_s.at[p], q_r.at[p], p, e).wait_recv()
    target = moves[e, d]
    q0 = jnp.zeros(q_send.shape, F32)
    for j in range(dp):
        q0 += jnp.where(target == j, q_recv[j].astype(F32), 0.0)
    att = attend(0, q0)
    for k in range(ex):
        a0_send[k] = att[k * hk : (k + 1) * hk]

    def a0_copy(o, source):
        p = lax.rem(me + o, n)
        pd, pk = p // ex, lax.rem(p, ex)
        sd, sk = (d, e) if not source else (pd, pk)
        slot = me if not source else p
        return copy(
            a0_send.at[pk], a0_recv.at[sd, sk], a0_s.at[p], a0_r.at[slot], pd, pk
        )

    def a0_start(o, c):
        a0_copy(o, False).start()
        return c

    lax.fori_loop(1, n, a0_start, 0)
    a0_recv[d, e] = a0_send[e]

    for o in range(1, ex):
        p = lax.rem(e + o, ex)
        copy(
            r_send.at[p], r_recv.at[pl.ds(p * rows, rows)], r_s.at[p], r_r.at[p], d, p
        ).wait_recv()
        copy(
            a_send.at[p],
            a_recv.at[pl.ds(p * rows + 1, rows - 1)],
            a_s.at[p],
            a_r.at[p],
            d,
            p,
        ).wait_recv()

    def a0_wait(o, c):
        a0_copy(o, True).wait_recv()
        return c

    local[1].wait()
    lax.fori_loop(1, n, a0_wait, 0)
    for k in range(ex):
        chosen = jnp.zeros((hk, HD), F32)
        for j in range(dp):
            chosen += jnp.where(moves[k, j] == d, a0_recv[j, k], 0.0)
        a_recv[k * rows] = chosen
    for h in range(hk):
        a_all[:, h * HD : (h + 1) * HD] = a_recv[:, h, :].astype(BF16)

    def project(k):
        return jnp.dot(
            a_all[...],
            wo[:, pl.ds(pl.multiple_of(k * part, HD), part)],
            preferred_element_type=F32,
        )

    for o in range(1, ex):
        p = lax.rem(e + o, ex)
        p_send[p] = project(p).astype(BF16)
        c = copy(p_send.at[p], p_recv.at[e], p_s.at[p], p_r.at[e], d, p)
        c.start()
        sends.append(c)
    hid[...] = project(e)
    for j in range(tiles):
        hid[:, j * HD : (j + 1) * HD] += r_recv[:, j, :]
    for o in range(1, ex):
        p = lax.rem(e + o, ex)
        copy(p_send.at[p], p_recv.at[p], p_s.at[p], p_r.at[p], d, p).wait_recv()
        hid[...] += p_recv[p].astype(F32)

    hidden = hid[...]
    squares = jnp.sum(hidden * hidden, axis=-1, keepdims=True)
    last = lax.broadcasted_iota(jnp.int32, (tokens, HD), 1) == HD - 1
    s_send[...] = jnp.where(last, squares, r_recv[:, tiles, :])
    x_send[...] = (
        hidden * gain[:, pl.ds(pl.multiple_of(e * part, HD), part)]
    ).astype(BF16)

    core = lax.rem(d, 2)
    chip = d // 2
    chips = dp // 2
    twin = d + 1 - 2 * core

    def x_at(dd, ee):
        return x_all.at[
            pl.ds(pl.multiple_of(dd * tokens, 16), tokens),
            pl.ds(pl.multiple_of(ee * part, HD), part),
        ]

    def x_twin(dd, ee, to):
        return copy(
            x_at(dd, ee), x_at(dd, ee), x2_s.at[dd, ee], x2_r.at[dd, ee], to, e
        )

    def x_chip(p, dd, ee):
        to = p * 2 + core
        return copy(
            x_at(dd, ee), x_at(dd, ee), x3_s.at[p, ee], x2_r.at[dd, ee], to, e
        )

    def spread(ee):
        made = [x_chip(lax.rem(chip + o, chips), d, ee) for o in range(1, chips)]
        made.append(x_twin(d, ee, twin))
        for c in made:
            c.start()
        sends.extend(made)

    exchange(ex, e, lambda p: copy(x_send, x_at(d, e), x_s.at[p], x_r.at[e], d, p))
    exchange(ex, e, lambda p: copy(s_send, s_part.at[e], s_s.at[p], s_r.at[e], d, p))
    x_at(d, e)[...] = x_send[...]
    spread(e)
    s_part[e] = s_send[...]
    for o in range(1, ex):
        p = lax.rem(e + o, ex)
        copy(x_send, x_at(d, p), x_s.at[p], x_r.at[p], d, p).wait_recv()
        spread(p)
    for o in range(1, ex):
        p = lax.rem(e + o, ex)
        copy(s_send, s_part.at[p], s_s.at[p], s_r.at[p], d, p).wait_recv()
    square_sum = s_part[0]
    for k in range(1, ex):
        square_sum += s_part[k]
    s_all[d] = jnp.where(
        last, lax.rsqrt(square_sum / width + NORM_EPS), r_recv[:, tiles, :]
    )
    exchange(
        dp, d, lambda p: copy(s_all.at[d], s_all.at[d], s2_s.at[p], s2_r.at[d], p, e)
    )

    local[2].wait()
    local[3].wait()
    every = dp * tokens
    for o in range(ex):
        k = lax.rem(e + o, ex)
        for q in range(1, chips):
            p = lax.rem(chip + q, chips)
            dd = p * 2 + core
            x_chip(p, dd, k).wait_recv()
            c = x_twin(dd, k, twin)
            c.start()
            sends.append(c)
        for q in range(chips):
            x_twin(lax.rem(chip + q, chips) * 2 + 1 - core, k, twin).wait_recv()
        block = x_all[:, pl.ds(pl.multiple_of(k * part, HD), part)]
        lines = pl.ds(pl.multiple_of(k * part, 16), part)
        g = jnp.dot(block, wg[lines, :], preferred_element_type=F32)
        u = jnp.dot(block, wu[lines, :], preferred_element_type=F32)
        gate_sum[...] = g if o == 0 else gate_sum[...] + g
        up_sum[...] = u if o == 0 else up_sum[...] + u
    for o in range(1, dp):
        p = lax.rem(d + o, dp)
        copy(s_all.at[p], s_all.at[p], s2_s.at[p], s2_r.at[p], p, e).wait_recv()
    wide_lane = lax.broadcasted_iota(jnp.int32, (every, HD), 1)
    stats = s_all[...].reshape(every, HD)
    weight = jnp.sum(jnp.where(wide_lane == d, stats, 0.0), axis=-1, keepdims=True)
    scale = stats[:, HD - 1 :]
    gate_val = gate_sum[...] * scale
    act = (gate_val / (1.0 + jnp.exp(-gate_val)) * (up_sum[...] * scale)).astype(BF16)

    local[4].wait()

    def y_twin(c):
        cols = pl.ds(c * part, part)
        return copy(
            y_send.at[1 - core, :, :, cols],
            y_recv.at[:, :, cols],
            y_s.at[c],
            y_r.at[c],
            twin,
            e,
        )

    def v_copy(p, src, c):
        cols = pl.ds(c * part, part)
        return copy(
            v_send.at[p, :, cols],
            v_recv.at[src, :, cols],
            v_s.at[c, p],
            v_r.at[c, src],
            p * 2 + core,
            e,
        )

    def z_copy(p, src, c):
        return copy(
            z_send.at[c, p], z_recv.at[c, src], z_s.at[c, p], z_r.at[c, src], d, p
        )

    def down(c):
        y = jnp.dot(
            act, wd[:, c * part : (c + 1) * part], preferred_element_type=F32
        ) * weight
        for dd in range(dp):
            y_send[dd % 2, dd // 2, :, c * part : (c + 1) * part] = y[
                dd * tokens : (dd + 1) * tokens
            ].astype(BF16)
        t = y_twin(c)
        t.start()
        sends.append(t)

    def over_cores(c):
        cols = slice(c * part, (c + 1) * part)
        y_twin(c).wait_recv()
        for o in range(1, chips):
            p = lax.rem(chip + o, chips)
            v_send[p, :, cols] = (
                y_send[core, p, :, cols].astype(F32) + y_recv[p, :, cols].astype(F32)
            ).astype(BF16)
            t = v_copy(p, chip, c)
            t.start()
            sends.append(t)

    def over_chips(c):
        cols = slice(c * part, (c + 1) * part)
        got = y_send[core, chip, :, cols].astype(F32) + y_recv[chip, :, cols].astype(F32)
        got += jnp.where(e == c, hid[...], 0.0)
        for o in range(1, chips):
            p = lax.rem(chip + o, chips)
            v_copy(p, p, c).wait_recv()
            got += v_recv[p, :, cols].astype(F32)
        total[...] = got
        for k in range(ex):
            for i in range(pieces):
                fold[c, k, i * rows : (i + 1) * rows, :] = total[
                    k * rows : (k + 1) * rows, i * piece : (i + 1) * piece
                ]
            z_send[c, k] = fold[c, k].astype(BF16)
        exchange(ex, e, lambda p: z_copy(p, e, c))

    for c in range(ex):
        down(c)
        if c:
            over_cores(c - 1)
    over_cores(ex - 1)
    for c in range(ex):
        over_chips(c)
    for c in range(ex):
        result = fold[c, e]
        for o in range(1, ex):
            p = lax.rem(e + o, ex)
            z_copy(p, p, c).wait_recv()
            result += z_recv[c, p].astype(F32)
        for i in range(pieces):
            out[:, c * part + i * piece : c * part + (i + 1) * piece] = result[
                i * rows : (i + 1) * rows
            ].astype(out.dtype)

    for c in sends:
        c.wait_send()

    def a0_sent(o, c):
        a0_copy(o, False).wait_send()
        return c

    lax.fori_loop(1, n, a0_sent, 0)


def per_device(
    query,
    fresh_kv,
    cache,
    lengths,
    moves,
    residual,
    out_weight,
    norm_gain,
    w_gate,
    w_up,
    w_down,
    routes,
    gates,
):
    dp = lax.axis_size("dp")
    ex = lax.axis_size("expert")
    n = dp * ex
    rows, width = query.shape
    heads = width // HD
    hk = heads // ex
    part = width // ex
    tiles = part // HD
    tokens = rows * ex
    ff = w_gate.shape[-1]
    pieces = 16 // rows
    qrows = -(-(heads + 2 * KVH) // 16) * 16
    dma = pltpu.SemaphoreType.DMA
    vmem = pltpu.VMEM
    scratch = [
        vmem(cache.shape, BF16),
        vmem(out_weight.shape, BF16),
        vmem((width, ff), BF16),
        vmem((width, ff), BF16),
        vmem((ff, width), BF16),
        vmem((rows, qrows, HD), F32),
        vmem((qrows, HD), BF16),
        vmem((dp, qrows, HD), BF16),
        vmem((ex, rows, tiles + 1, HD), F32),
        vmem((tokens, tiles + 1, HD), F32),
        vmem((ex, rows - 1, hk, HD), F32),
        vmem((ex, hk, HD), F32),
        vmem((dp, ex, hk, HD), F32),
        vmem((tokens, hk, HD), F32),
        vmem((tokens, part), BF16),
        vmem((ex, tokens, part), BF16),
        vmem((ex, tokens, part), BF16),
        vmem((tokens, part), F32),
        vmem((tokens, part), BF16),
        vmem((tokens, HD), F32),
        vmem((ex, tokens, HD), F32),
        vmem((dp * tokens, width), BF16),
        vmem((dp, tokens, HD), F32),
        vmem((dp * tokens, ff), F32),
        vmem((dp * tokens, ff), F32),
        vmem((2, dp // 2, tokens, width), BF16),
        vmem((dp // 2, tokens, width), BF16),
        vmem((dp // 2, tokens, width), BF16),
        vmem((dp // 2, tokens, width), BF16),
        vmem((tokens, part), F32),
        vmem((ex, ex, 16, part // pieces), F32),
        vmem((ex, ex, 16, part // pieces), BF16),
        vmem((ex, ex, 16, part // pieces), BF16),
        dma((5,)),
    ]
    for shape in ((dp,), (ex,), (ex,), (n,), (ex,), (ex,), (ex,), (dp, ex)):
        scratch += [dma(shape), dma(shape)]
    scratch.append(dma((dp // 2, ex)))
    for shape in ((dp,), (ex,), (ex, dp // 2), (ex, ex)):
        scratch += [dma(shape), dma(shape)]
    smem = pl.BlockSpec(memory_space=pltpu.SMEM)
    inside = pl.BlockSpec(memory_space=pltpu.VMEM)
    outside = pl.BlockSpec(memory_space=pl.ANY)
    return pl.pallas_call(
        functools.partial(layer_kernel, dp, ex),
        out_shape=jax.ShapeDtypeStruct(query.shape, BF16),
        in_specs=[smem] * 4 + [inside] * 4 + [outside] * 5,
        out_specs=inside,
        scratch_shapes=scratch,
        compiler_params=pltpu.CompilerParams(
            collective_id=0,
            has_side_effects=True,
            vmem_limit_bytes=56 * 1024 * 1024,
        ),
    )(
        lengths,
        moves,
        routes.T,
        gates.T,
        query,
        fresh_kv,
        residual,
        norm_gain.reshape(1, width),
        cache,
        out_weight,
        w_gate,
        w_up,
        w_down,
    )


def solution(mesh):
    placed = (
        P(("groups", "dp", "expert"), None),
        P(("groups", "dp", "expert"), None),
        P(("groups", "dp", "expert"), None, None),
        P(("groups", "dp", "expert")),
        P("groups", None),
        P(("groups", "dp", "expert"), None),
        P("expert", None),
        P(),
        P("dp", None, "expert"),
        P("dp", None, "expert"),
        P("dp", "expert", None),
        P(("groups", "dp", "expert"), None),
        P(("groups", "dp", "expert"), None),
    )
    return jax.shard_map(
        per_device,
        mesh=mesh,
        in_specs=placed,
        out_specs=P(("groups", "dp", "expert"), None),
        check_vma=False,
    )
```
